32 devices in a mesh: wide: 8 (over y, x, core), narrow: 4 (over z).
Axes of the slice: x: 2, y: 2, z: 4, core: 2. Of those that a mesh axis runs over, the one named last changes fastest.
Arguments:
- corr_panel: float32 [4096, 512], P('wide', 'narrow'), may hold values from -24 to 24
- factor_prev: float32 [4096, 1024], P('wide', 'narrow'), may hold values from -400 to 400
- draws_prev: float32 [1024, 32], P('narrow'), may hold values from -6 to 6
- draws_panel: float32 [512, 32], P('narrow'), may hold values from -6 to 6
- diag_inverse: float32 [512, 512], P('narrow'), may hold values from -1 to 1, as said below
Outputs:
- panel_factor: float32 [4096, 512], P('wide', 'narrow')
- smoothed: float32 [32, 4096], P(('narrow', 'wide'))
The draws below stay inside these ranges and needn't reach their ends.
Inputs may be any that keep to these rules, and one draw needn't show every extreme that they name: `diag_inverse`: lower triangular with a positive diagonal.
All inputs are finite; a program needn't handle non-finite values.
Results may differ from the reference program's by a relative error of at most 0.0003.
Values sent between devices are 32-bit elements; how exact they have to be, the bound alone decides.
No kernel may reach another device: no remote copies, remote signals or barrier semaphores. Data moves between devices by JAX's collectives and lax.ppermute only.
A program may use at most 64 MiB of HBM per device.

```python
import math
import jax
import jax.numpy as jnp
from jax import lax

PANEL = 512
WIN = 5
N = 4096
K = 1024
S = 32


def draw_factor_prev(key, part):
    row_key, col_key, value_key = jax.random.split(key, 3)
    col_ramp = jnp.arange(K, dtype=jnp.float32) / K
    row_scale = jnp.exp(jax.random.uniform(row_key, (N, 1), jnp.float32) * math.log(10.0))
    col_scale = jnp.exp(col_ramp * math.log(3.0) + jax.random.uniform(col_key, (K,), jnp.float32) * math.log(2.0))
    values = jax.random.truncated_normal(value_key, -5.0, 5.0, (N, K), jnp.float32)
    return values * row_scale * col_scale[None, :] * K ** (-0.25)


def draw_diag_inverse(key, part):
    off_key, diag_key = jax.random.split(key)
    off_values = jax.random.truncated_normal(off_key, -5.0, 5.0, (PANEL, PANEL), jnp.float32)
    diag_values = jax.random.uniform(diag_key, (PANEL,), jnp.float32, 0.05, 0.15)
    lower_part = jnp.tril(off_values, -1) * (0.1 / math.sqrt(PANEL))
    return lower_part + jnp.diag(diag_values)


def levels(own_key, shape, cuts, smallest, high):
    loudness, own = 1.0, jax.random.fold_in(own_key, 6)
    for axis_at, parts in cuts:
        steps = jnp.exp(jax.random.uniform(jax.random.fold_in(own, axis_at), (parts,), jnp.float32, smallest / len(cuts), high / len(cuts)))
        loudness = loudness * jnp.repeat(steps, shape[axis_at] // parts).reshape([-1 if axis == axis_at else 1 for axis in range(len(shape))])
    return loudness


def scatter_about(rng, extent, scale, most, pieces=(), kind=jnp.bfloat16):
    gain = levels(rng, extent, pieces, -0.22, 0.18) if pieces else 1.0
    entries = jax.random.normal(rng, extent, jnp.float32) * scale * gain
    return jnp.minimum(jnp.maximum(entries, -most), most).astype(kind)


def setup_inputs(seed: int = 0) -> dict:
    key_of = jax.random.split(jax.random.key(seed), 6)
    corr_panel = scatter_about(key_of[0], (N, PANEL), 4.0, 24.0, ((0, 8), (1, 4)), jnp.float32)
    factor_prev = draw_factor_prev(jax.random.fold_in(key_of[5], 71), 0)
    draws_prev = scatter_about(key_of[2], (K, S), 1.0, 6.0, ((0, 4),), jnp.float32)
    draws_panel = scatter_about(key_of[3], (PANEL, S), 1.0, 6.0, ((0, 4),), jnp.float32)
    diag_inverse = draw_diag_inverse(jax.random.fold_in(key_of[5], 71), 0)
    return {"corr_panel": corr_panel, "factor_prev": factor_prev, "draws_prev": draws_prev, "draws_panel": draws_panel, "diag_inverse": diag_inverse}


def smooth(uniforms):
    half_span = (WIN - 1) // 2
    feature_count = uniforms.shape[1]
    padded = jnp.pad(uniforms, ((0, 0), (half_span, half_span)))
    summed = jnp.zeros_like(uniforms)
    for offset in range(WIN):
        weight_tap = math.comb(WIN - 1, offset) / 2.0 ** (WIN - 1)
        summed = summed + weight_tap * padded[:, offset:offset + feature_count]
    return summed

def reference(corr_panel, factor_prev, draws_prev, draws_panel, diag_inverse):
    exact_mode = lax.Precision.HIGHEST
    pivot_block = factor_prev[K:K + PANEL, :]
    updated = corr_panel - jnp.dot(factor_prev, pivot_block.T, precision=exact_mode, preferred_element_type=jnp.float32)
    panel_factor = jnp.dot(updated, diag_inverse.T, precision=exact_mode, preferred_element_type=jnp.float32)
    samples = jnp.dot(draws_prev.T, factor_prev.T, precision=exact_mode, preferred_element_type=jnp.float32)
    samples = samples + jnp.dot(draws_panel.T, panel_factor.T, precision=exact_mode, preferred_element_type=jnp.float32)
    variance = lax.optimization_barrier(jnp.sum(factor_prev * factor_prev, axis=1)) + lax.optimization_barrier(jnp.sum(panel_factor * panel_factor, axis=1))
    scaled = samples * lax.rsqrt(variance + 1e-06)[None, :]
    uniforms = 0.5 * (1.0 + lax.erf(scaled * (1.0 / math.sqrt(2.0))))
    return (panel_factor, smooth(uniforms))
```

```python
import math

import jax
import jax.numpy as jnp
from jax import lax
from jax.sharding import PartitionSpec as P

WIN = 5
PRECISE = lax.Precision.HIGH
HALF_ROOT = 1.0 / math.sqrt(2.0)


def contract(left_side, right_side, left_dim, right_dim):
    return lax.dot_general(
        left_side,
        right_side,
        (((left_dim,), (right_dim,)), ((), ())),
        precision=PRECISE,
        preferred_element_type=jnp.float32,
    )


def broadcast(value, size, source):
    place = lax.axis_index("wide")
    holders = [source]
    held = jnp.where(place == source, value, 0.0)
    shift = 1
    while (1 << shift) < size:
        flips = [f << shift for f in (1, 2, 3) if (f << shift) < size]
        arrived = [lax.ppermute(held, "wide", [(h, h ^ f) for h in holders]) for f in flips]
        for block in arrived:
            held = held + block
        holders = holders + [h ^ f for h in holders for f in flips]
        shift += 2
    other = lax.ppermute(held, "wide", [(h, h ^ 1) for h in holders])
    return held + other


def smooth(uniforms):
    half_span = (WIN - 1) // 2
    feature_count = uniforms.shape[1]
    padded = jnp.pad(uniforms, ((0, 0), (half_span, half_span)))
    summed = jnp.zeros_like(uniforms)
    for offset in range(WIN):
        weight_tap = math.comb(WIN - 1, offset) / 2.0 ** (WIN - 1)
        summed = summed + weight_tap * padded[:, offset : offset + feature_count]
    return summed


def per_device(wide, narrow, corr_panel, factor_prev, draws_prev, draws_panel, diag_inverse):
    row_count, depth = factor_prev.shape
    col_share = corr_panel.shape[1]
    narrow_place = lax.axis_index("narrow")

    pivot = broadcast(factor_prev, wide, depth * narrow // row_count)
    diag = [diag_inverse] + [
        lax.ppermute(diag_inverse, "narrow", [(i, (i + k) % narrow) for i in range(narrow)])
        for k in range(1, narrow)
    ]

    parts = []
    for rows in diag:
        mixed = contract(rows, pivot, 1, 0)
        own_cols = lax.dynamic_slice_in_dim(rows, narrow_place * col_share, col_share, 1)
        parts.append(contract(corr_panel, own_cols, 1, 1) - contract(factor_prev, mixed, 1, 1))
    panel_factor = parts[0]
    for k in range(1, narrow):
        panel_factor = panel_factor + lax.ppermute(
            parts[k], "narrow", [(i, (i - k) % narrow) for i in range(narrow)]
        )

    samples = contract(draws_prev, factor_prev, 0, 1) + contract(draws_panel, panel_factor, 0, 1)
    squares = jnp.sum(factor_prev * factor_prev, axis=1) + jnp.sum(panel_factor * panel_factor, axis=1)
    outgoing = jnp.stack([samples, jnp.broadcast_to(squares[None, :], samples.shape)], axis=1)
    incoming = lax.all_to_all(outgoing, ("narrow", "wide"), split_axis=0, concat_axis=0, tiled=True)
    whole = jnp.sum(incoming.reshape(narrow, wide, 2, row_count), axis=0)
    scaled = whole[:, 0] * lax.rsqrt(whole[:, 1] + 1e-06)
    uniforms = 0.5 * (1.0 + lax.erf(scaled * HALF_ROOT))
    return (panel_factor, smooth(uniforms.reshape(1, wide * row_count)))


def solution(mesh):
    wide, narrow = mesh.shape["wide"], mesh.shape["narrow"]
    in_specs = (
        P("wide", "narrow"),
        P("wide", "narrow"),
        P("narrow", None),
        P("narrow", None),
        P("narrow", None),
    )
    out_specs = (P("wide", "narrow"), P(("narrow", "wide"), None))

    def body(*blocks):
        return per_device(wide, narrow, *blocks)

    return jax.shard_map(body, mesh=mesh, in_specs=in_specs, out_specs=out_specs, check_vma=False)
```

```python
import math

import jax
import jax.numpy as jnp
from jax import lax
from jax.sharding import PartitionSpec as P

WIN = 5
PRECISE = lax.Precision.HIGH
HALF_ROOT = 1.0 / math.sqrt(2.0)


def contract(left_side, right_side, left_dim, right_dim):
    return lax.dot_general(
        left_side,
        right_side,
        (((left_dim,), (right_dim,)), ((), ())),
        precision=PRECISE,
        preferred_element_type=jnp.float32,
    )


def broadcast(value, size, source):
    place = lax.axis_index("wide")
    holders = [source]
    held = jnp.where(place == source, value, 0.0)
    shift = 1
    while (1 << shift) < size:
        flips = [f << shift for f in (1, 2, 3) if (f << shift) < size]
        arrived = [lax.ppermute(held, "wide", [(h, h ^ f) for h in holders]) for f in flips]
        for block in arrived:
            held = held + block
        holders = holders + [h ^ f for h in holders for f in flips]
        shift += 2
    return held, holders


def smooth(uniforms):
    half_span = (WIN - 1) // 2
    feature_count = uniforms.shape[1]
    padded = jnp.pad(uniforms, ((0, 0), (half_span, half_span)))
    summed = jnp.zeros_like(uniforms)
    for offset in range(WIN):
        weight_tap = math.comb(WIN - 1, offset) / 2.0 ** (WIN - 1)
        summed = summed + weight_tap * padded[:, offset : offset + feature_count]
    return summed


def per_device(wide, narrow, corr_panel, factor_prev, draws_prev, draws_panel, diag_inverse):
    row_count, depth = factor_prev.shape
    col_share = corr_panel.shape[1]
    half = diag_inverse.shape[0] // 2
    wide_place, narrow_place = lax.axis_index("wide"), lax.axis_index("narrow")
    core = wide_place % 2
    swap = [(i, i ^ 1) for i in range(wide)]

    def below(value, k):
        return lax.ppermute(value, "narrow", [(i, (i - k) % narrow) for i in range(narrow)])

    def above(value, k):
        return lax.ppermute(value, "narrow", [(i, (i + k) % narrow) for i in range(narrow)])

    held, holders = broadcast(factor_prev, wide, depth * narrow // row_count)
    own_half = lax.dynamic_slice_in_dim(diag_inverse, core * half, half, 0)
    halves = [above(own_half, k) for k in range(1, narrow)]
    held, *halves = lax.optimization_barrier((held, *halves))
    pivot = held + lax.ppermute(held, "wide", [(h, h ^ 1) for h in holders])
    mine = jnp.stack(halves)
    other = lax.ppermute(mine, "wide", swap)
    fetched = jnp.where(core == 0, jnp.concatenate([mine, other], 1), jnp.concatenate([other, mine], 1))
    diag = [diag_inverse] + [fetched[k] for k in range(narrow - 1)]

    def part(k):
        mixed = contract(diag[k], pivot, 1, 0)
        own_cols = lax.dynamic_slice_in_dim(diag[k], narrow_place * col_share, col_share, 1)
        return contract(corr_panel, own_cols, 1, 1) - contract(factor_prev, mixed, 1, 1)

    arrived = [below(part(k), k) for k in range(narrow - 1, 0, -1)]
    panel_factor = part(0)
    for block in arrived:
        panel_factor = panel_factor + block

    samples = contract(draws_prev, factor_prev, 0, 1) + contract(draws_panel, panel_factor, 0, 1)
    squares = jnp.sum(factor_prev * factor_prev, axis=1) + jnp.sum(panel_factor * panel_factor, axis=1)
    share = samples.shape[0] // narrow
    blocks = jnp.concatenate(
        [
            samples.reshape(narrow, share, row_count),
            jnp.broadcast_to(squares[None, None, :], (narrow, 1, row_count)),
        ],
        axis=1,
    )

    def block_below(k):
        return lax.dynamic_index_in_dim(blocks, (narrow_place - k) % narrow, 0, keepdims=False)

    summed = block_below(0)
    for block in [below(block_below(k), k) for k in range(1, narrow)]:
        summed = summed + block
    scaled = summed[:share] * lax.rsqrt(summed[share:] + 1e-06)
    uniforms = 0.5 * (1.0 + lax.erf(scaled * HALF_ROOT))
    whole = lax.all_to_all(uniforms, "wide", split_axis=0, concat_axis=1, tiled=True)
    return (panel_factor, smooth(whole))


def solution(mesh):
    wide, narrow = mesh.shape["wide"], mesh.shape["narrow"]
    in_specs = (
        P("wide", "narrow"),
        P("wide", "narrow"),
        P("narrow", None),
        P("narrow", None),
        P("narrow", None),
    )
    out_specs = (P("wide", "narrow"), P(("narrow", "wide"), None))

    def body(*blocks):
        return per_device(wide, narrow, *blocks)

    return jax.shard_map(body, mesh=mesh, in_specs=in_specs, out_specs=out_specs, check_vma=False)
```

```python
import math

import jax
import jax.numpy as jnp
from jax import lax
from jax.sharding import PartitionSpec as P

WIN = 5
PRECISE = lax.Precision.HIGH
HALF_ROOT = 1.0 / math.sqrt(2.0)


def contract(left_side, right_side, left_dim, right_dim):
    return lax.dot_general(
        left_side,
        right_side,
        (((left_dim,), (right_dim,)), ((), ())),
        precision=PRECISE,
        preferred_element_type=jnp.float32,
    )


def pack(block, width):
    groups = width // block.shape[1]
    return jnp.concatenate(jnp.split(block, groups, 0), 1)


def unpack(packed, depth):
    return jnp.concatenate(jnp.split(packed, packed.shape[1] // depth, 1), 0)


def broadcast(block, source, wide, narrow, riders):
    place = lax.axis_index("wide")
    on_core = place % 2 == source % 2
    riders, carried = list(riders), []
    half = block.shape[0] // 2
    top = jnp.where(place == source, pack(block[:half], wide_of(riders)), 0.0)
    bottom = jnp.where(place == source, pack(block[half:], wide_of(riders)), 0.0)
    holders = [source]

    def pairs(flips):
        return [
            ((h ^ fro) * narrow + i, (h ^ to) * narrow + i)
            for h in holders
            for fro, to in flips
            for i in range(narrow)
        ]

    def send(*loads):
        values, routes = [], []
        for value, flips in loads:
            route = pairs(flips)
            if riders:
                rider, more = riders.pop(0)
                value, route = jnp.where(on_core, value, rider), route + more
            values.append(value)
            routes.append(route)
        values = lax.optimization_barrier(tuple(values))
        return [lax.ppermute(v, ("wide", "narrow"), r) for v, r in zip(values, routes)]

    shift = 1
    while (1 << shift) < wide:
        low, high = 1 << shift, 2 << shift
        if high < wide:
            both = low | high
            more = len(riders) > 0
            to_low, to_high = send((top, [(0, low)]), (bottom, [(0, high)]))
            carried += [to_low, to_high] if more else []
            top, bottom = top + to_low, bottom + to_high
            more = len(riders) > 0
            (to_high,) = send((top, [(0, high), (low, both)]))
            carried += [to_high] if more else []
            (to_low,) = send((bottom, [(0, low), (high, both)]))
            top, bottom = top + to_high, bottom + to_low
            holders = [h ^ f for h in holders for f in (0, low, high, both)]
        else:
            to_low = send((top, [(0, low)]), (bottom, [(0, low)]))
            top, bottom = top + to_low[0], bottom + to_low[1]
            holders = [h ^ f for h in holders for f in (0, low)]
        shift += 2
    return top, bottom, carried


def wide_of(riders):
    return riders[0][0].shape[1]


def smooth(uniforms):
    half_span = (WIN - 1) // 2
    feature_count = uniforms.shape[1]
    padded = jnp.pad(uniforms, ((0, 0), (half_span, half_span)))
    summed = jnp.zeros_like(uniforms)
    for offset in range(WIN):
        weight_tap = math.comb(WIN - 1, offset) / 2.0 ** (WIN - 1)
        summed = summed + weight_tap * padded[:, offset : offset + feature_count]
    return summed


def per_device(wide, narrow, corr_panel, factor_prev, draws_prev, draws_panel, diag_inverse):
    row_count, depth = factor_prev.shape
    col_share, panel = diag_inverse.shape
    narrow_place = lax.axis_index("narrow")
    source = depth * narrow // row_count
    on_core = lax.axis_index("wide") % 2 == source % 2
    fetchers = [c for c in range(wide) if c % 2 != source % 2]

    def shifted(k):
        return [(c * narrow + i, c * narrow + (i + k) % narrow) for c in fetchers for i in range(narrow)]

    order = sorted(range(1, narrow), key=lambda k: (abs(2 * k - narrow), -k))
    top, bottom, rows = broadcast(
        factor_prev, source, wide, narrow, [(diag_inverse, shifted(k)) for k in range(narrow - 1, 0, -1)]
    )
    rows = [rows[narrow - 1 - k] for k in order]
    own_pivot, own_rows = jnp.concatenate([top, bottom]), jnp.concatenate(rows)
    spare = own_rows.shape[0] - own_pivot.shape[0]
    pieces = jnp.where(on_core, jnp.pad(own_pivot, ((0, spare), (0, 0))), own_rows)
    swapped = lax.ppermute(pieces, "wide", [(i, i ^ 1) for i in range(wide)])
    own_pivot, swapped_pivot = pieces[: own_pivot.shape[0]], swapped[: own_pivot.shape[0]]
    pivot = jnp.where(on_core, own_pivot, swapped_pivot)
    pivot = jnp.concatenate([unpack(half, depth) for half in jnp.split(pivot, 2)])

    def part(diag):
        mixed = contract(diag, pivot, 1, 0)
        own_cols = lax.dynamic_slice_in_dim(diag, narrow_place * col_share, col_share, 1)
        return contract(corr_panel, own_cols, 1, 1) - contract(factor_prev, mixed, 1, 1)

    def deliver(value, k):
        return lax.ppermute(value, "narrow", [(i, (i - k) % narrow) for i in range(narrow)])

    arrived = []
    for at, k in enumerate(order):
        at = slice(at * col_share, (at + 1) * col_share)
        arrived.append(deliver(part(jnp.where(on_core, swapped[at], pieces[at])), k))
    panel_factor = part(diag_inverse)
    for block in arrived:
        panel_factor = panel_factor + block

    samples = contract(draws_prev, factor_prev, 0, 1) + contract(draws_panel, panel_factor, 0, 1)
    squares = jnp.sum(factor_prev * factor_prev, axis=1) + jnp.sum(panel_factor * panel_factor, axis=1)
    outgoing = jnp.concatenate([samples, jnp.broadcast_to(squares[None, :], samples.shape)], axis=1)
    incoming = lax.all_to_all(outgoing, ("narrow", "wide"), split_axis=0, concat_axis=0, tiled=True)
    whole = jnp.sum(incoming.reshape(narrow, wide, 2 * row_count), axis=0)
    scaled = whole[:, :row_count] * lax.rsqrt(whole[:, row_count:] + 1e-06)
    uniforms = 0.5 * (1.0 + lax.erf(scaled * HALF_ROOT))
    return (panel_factor, smooth(uniforms.reshape(1, wide * row_count)))


def solution(mesh):
    wide, narrow = mesh.shape["wide"], mesh.shape["narrow"]
    in_specs = (
        P("wide", "narrow"),
        P("wide", "narrow"),
        P("narrow", None),
        P("narrow", None),
        P("narrow", None),
    )
    out_specs = (P("wide", "narrow"), P(("narrow", "wide"), None))

    def body(*blocks):
        return per_device(wide, narrow, *blocks)

    return jax.shard_map(body, mesh=mesh, in_specs=in_specs, out_specs=out_specs, check_vma=False)
```

```python
import math

import jax
import jax.numpy as jnp
from jax import lax
from jax.sharding import PartitionSpec as P

WIN = 5
PRECISE = lax.Precision.HIGH
HALF_ROOT = 1.0 / math.sqrt(2.0)


def contract(left_side, right_side, left_dim, right_dim):
    return lax.dot_general(
        left_side,
        right_side,
        (((left_dim,), (right_dim,)), ((), ())),
        precision=PRECISE,
        preferred_element_type=jnp.float32,
    )


def pack(block, width):
    groups = width // block.shape[1]
    return jnp.concatenate(jnp.split(block, groups, 0), 1)


def unpack(packed, depth):
    return jnp.concatenate(jnp.split(packed, packed.shape[1] // depth, 1), 0)


def broadcast(block, source, wide, narrow, riders):
    place = lax.axis_index("wide")
    on_core = place % 2 == source % 2
    riders, carried = list(riders), []
    packed = pack(block, riders[0][0].shape[1])
    half = packed.shape[0] // 2
    held = jnp.where(place == source, packed, 0.0)
    holders = [source]

    def send(value, to):
        pairs = [(h * narrow + i, (h ^ to) * narrow + i) for h in holders for i in range(narrow)]
        if not riders or value.shape != riders[0][0].shape:
            return lax.ppermute(value, ("wide", "narrow"), pairs)
        rider, more = riders.pop(0)
        carried.append(lax.ppermute(jnp.where(on_core, value, rider), ("wide", "narrow"), pairs + more))
        return carried[-1]

    shift = 1
    while (1 << shift) < wide:
        low, high, both = 1 << shift, 2 << shift, 3 << shift
        top, bottom = packed[:half], packed[half:]
        tops, bottoms = [send(top, low)], [send(bottom, low)]
        if high < wide:
            for flip in (both, high):
                tops.append(send(top, flip))
                bottoms.append(send(bottom, flip))
        held = held + jnp.concatenate([sum(tops), sum(bottoms)])
        holders = [h ^ f for h in holders for f in (0, low, high, both)[: 1 + len(tops)]]
        packed = held
        shift += 2
    return held, carried


def smooth(uniforms):
    half_span = (WIN - 1) // 2
    feature_count = uniforms.shape[1]
    padded = jnp.pad(uniforms, ((0, 0), (half_span, half_span)))
    summed = jnp.zeros_like(uniforms)
    for offset in range(WIN):
        weight_tap = math.comb(WIN - 1, offset) / 2.0 ** (WIN - 1)
        summed = summed + weight_tap * padded[:, offset : offset + feature_count]
    return summed


def per_device(wide, narrow, corr_panel, factor_prev, draws_prev, draws_panel, diag_inverse):
    row_count, depth = factor_prev.shape
    col_share, panel = diag_inverse.shape
    narrow_place = lax.axis_index("narrow")
    source = depth * narrow // row_count
    on_core = lax.axis_index("wide") % 2 == source % 2
    fetchers = [c for c in range(wide) if c % 2 != source % 2]

    def shifted(k):
        return [(c * narrow + i, c * narrow + (i + k) % narrow) for c in fetchers for i in range(narrow)]

    far = list(range(narrow - 1, 0, -1))
    own_pivot, rows = broadcast(
        factor_prev, source, wide, narrow, [(diag_inverse, shifted(k)) for k in far]
    )
    rows = dict(zip(far, lax.optimization_barrier(tuple(rows))))

    even = narrow_place % 2 == 0
    own_rows = jnp.concatenate(
        [rows[2], jnp.where(even, rows[1], rows[3]), jnp.where(even, rows[3], rows[1])]
    )
    spare = own_rows.shape[0] - own_pivot.shape[0]
    pieces = jnp.where(on_core, jnp.pad(own_pivot, ((0, spare), (0, 0))), own_rows)
    swapped = lax.ppermute(pieces, "wide", [(i, i ^ 1) for i in range(wide)])
    own_pivot, swapped_pivot = pieces[: own_pivot.shape[0]], swapped[: own_pivot.shape[0]]
    pivot = unpack(jnp.where(on_core, own_pivot, swapped_pivot), depth)

    def part(diag, pivot):
        mixed = contract(diag, pivot, 1, 0)
        own_cols = lax.dynamic_slice_in_dim(diag, narrow_place * col_share, col_share, 1)
        return contract(corr_panel, own_cols, 1, 1) - contract(factor_prev, mixed, 1, 1)

    def turn_part(t, pivot):
        at = slice(t * col_share, (t + 1) * col_share)
        return lax.optimization_barrier((part(jnp.where(on_core, swapped[at], pieces[at]), pivot), pivot))

    end = (narrow_place == 0) | (narrow_place == narrow - 1)
    two_on, pivot = turn_part(0, pivot)
    two_on = lax.ppermute(two_on, "narrow", [(0, 1), (1, 3), (2, 0), (3, 2)])
    across, pivot = turn_part(1, pivot)
    outer = lax.ppermute(across, "narrow", [(0, 3), (3, 0)])
    beside, pivot = turn_part(2, pivot)
    beside = lax.ppermute(beside, "narrow", [(0, 1), (1, 0), (2, 3), (3, 2)])
    inner = lax.ppermute(across + two_on, "narrow", [(1, 2), (2, 1)])
    panel_factor = part(diag_inverse, pivot) + beside + outer + inner + jnp.where(end, two_on, 0.0)

    samples = contract(draws_prev, factor_prev, 0, 1) + contract(draws_panel, panel_factor, 0, 1)
    squares = jnp.sum(factor_prev * factor_prev, axis=1) + jnp.sum(panel_factor * panel_factor, axis=1)
    outgoing = jnp.concatenate([samples, jnp.broadcast_to(squares[None, :], samples.shape)], axis=1)
    incoming = lax.all_to_all(outgoing, ("narrow", "wide"), split_axis=0, concat_axis=0, tiled=True)
    whole = jnp.sum(incoming.reshape(narrow, wide, 2 * row_count), axis=0)
    scaled = whole[:, :row_count] * lax.rsqrt(whole[:, row_count:] + 1e-06)
    uniforms = 0.5 * (1.0 + lax.erf(scaled * HALF_ROOT))
    return (panel_factor, smooth(uniforms.reshape(1, wide * row_count)))


def solution(mesh):
    wide, narrow = mesh.shape["wide"], mesh.shape["narrow"]
    in_specs = (
        P("wide", "narrow"),
        P("wide", "narrow"),
        P("narrow", None),
        P("narrow", None),
        P("narrow", None),
    )
    out_specs = (P("wide", "narrow"), P(("narrow", "wide"), None))

    def body(*blocks):
        return per_device(wide, narrow, *blocks)

    return jax.shard_map(body, mesh=mesh, in_specs=in_specs, out_specs=out_specs, check_vma=False)
```

```python
import math

import jax
import jax.numpy as jnp
from jax import lax
from jax.sharding import PartitionSpec as P

WIN = 5
PRECISE = lax.Precision.HIGH
HALF_ROOT = 1.0 / math.sqrt(2.0)


def contract(left_side, right_side, left_dim, right_dim):
    return lax.dot_general(
        left_side,
        right_side,
        (((left_dim,), (right_dim,)), ((), ())),
        precision=PRECISE,
        preferred_element_type=jnp.float32,
    )


def pack(block, width):
    groups = width // block.shape[1]
    return jnp.concatenate(jnp.split(block, groups, 0), 1)


def unpack(packed, depth):
    return jnp.concatenate(jnp.split(packed, packed.shape[1] // depth, 1), 0)


def broadcast(block, source, wide, narrow, riders):
    place = lax.axis_index("wide")
    on_core = place % 2 == source % 2
    riders, carried = list(riders), []
    packed = pack(block, riders[0][0].shape[1])
    half = packed.shape[0] // 2
    held = jnp.where(place == source, packed, 0.0)
    holders = [source]

    def send(value, to):
        pairs = [(h * narrow + i, (h ^ to) * narrow + i) for h in holders for i in range(narrow)]
        if not riders or value.shape != riders[0][0].shape:
            return lax.ppermute(value, ("wide", "narrow"), pairs)
        rider, more = riders.pop(0)
        carried.append(lax.ppermute(jnp.where(on_core, value, rider), ("wide", "narrow"), pairs + more))
        return carried[-1]

    shift = 1
    while (1 << shift) < wide:
        low, high, both = 1 << shift, 2 << shift, 3 << shift
        top, bottom = packed[:half], packed[half:]
        tops, bottoms = [send(top, low)], [send(bottom, low)]
        if high < wide:
            for flip in (both, high):
                tops.append(send(top, flip))
                bottoms.append(send(bottom, flip))
        held = held + jnp.concatenate([sum(tops), sum(bottoms)])
        holders = [h ^ f for h in holders for f in (0, low, high, both)[: 1 + len(tops)]]
        packed = held
        shift += 2
    return held, carried


def smooth(uniforms):
    half_span = (WIN - 1) // 2
    feature_count = uniforms.shape[1]
    padded = jnp.pad(uniforms, ((0, 0), (half_span, half_span)))
    summed = jnp.zeros_like(uniforms)
    for offset in range(WIN):
        weight_tap = math.comb(WIN - 1, offset) / 2.0 ** (WIN - 1)
        summed = summed + weight_tap * padded[:, offset : offset + feature_count]
    return summed


def per_device(wide, narrow, corr_panel, factor_prev, draws_prev, draws_panel, diag_inverse):
    row_count, depth = factor_prev.shape
    col_share, panel = diag_inverse.shape
    narrow_place = lax.axis_index("narrow")
    source = depth * narrow // row_count
    on_core = lax.axis_index("wide") % 2 == source % 2
    fetchers = [c for c in range(wide) if c % 2 != source % 2]

    def shifted(k):
        return [(c * narrow + i, c * narrow + (i + k) % narrow) for c in fetchers for i in range(narrow)]

    far = list(range(narrow - 1, 0, -1))
    own_pivot, rows = broadcast(
        factor_prev, source, wide, narrow, [(diag_inverse, shifted(k)) for k in far]
    )
    rows = dict(zip(far, lax.optimization_barrier(tuple(rows))))

    draws = lax.optimization_barrier(jnp.concatenate([draws_prev, draws_panel]))
    samples_prev = contract(draws[:depth], factor_prev, 0, 1)

    even = narrow_place % 2 == 0
    own_rows = jnp.concatenate(
        [rows[2], jnp.where(even, rows[1], rows[3]), jnp.where(even, rows[3], rows[1])]
    )
    spare = own_rows.shape[0] - own_pivot.shape[0]
    pieces = jnp.where(on_core, jnp.pad(own_pivot, ((0, spare), (0, 0))), own_rows)
    swapped = lax.ppermute(pieces, "wide", [(i, i ^ 1) for i in range(wide)])
    own_pivot, swapped_pivot = pieces[: own_pivot.shape[0]], swapped[: own_pivot.shape[0]]
    pivot = unpack(jnp.where(on_core, own_pivot, swapped_pivot), depth)

    def part(diag, pivot):
        mixed = contract(diag, pivot, 1, 0)
        own_cols = lax.dynamic_slice_in_dim(diag, narrow_place * col_share, col_share, 1)
        return contract(corr_panel, own_cols, 1, 1) - contract(factor_prev, mixed, 1, 1)

    def turn_part(t, pivot):
        at = slice(t * col_share, (t + 1) * col_share)
        return lax.optimization_barrier((part(jnp.where(on_core, swapped[at], pieces[at]), pivot), pivot))

    end = (narrow_place == 0) | (narrow_place == narrow - 1)
    two_on, pivot = turn_part(0, pivot)
    two_on = lax.ppermute(two_on, "narrow", [(0, 1), (1, 3), (2, 0), (3, 2)])
    across, pivot = turn_part(1, pivot)
    beside, pivot = turn_part(2, pivot)
    across, beside = lax.optimization_barrier((across, beside))
    outer = lax.ppermute(across, "narrow", [(0, 3), (3, 0)])
    beside = lax.ppermute(beside, "narrow", [(0, 1), (1, 0), (2, 3), (3, 2)])
    inner = across + two_on
    inner, two_on, pivot = lax.optimization_barrier((inner, two_on, pivot))
    inner = lax.ppermute(inner, "narrow", [(1, 2), (2, 1)])
    parts = part(diag_inverse, pivot) + jnp.where(end, two_on, 0.0) + beside + outer
    panel_factor = lax.optimization_barrier(parts) + inner

    samples = samples_prev + contract(draws[depth:], panel_factor, 0, 1)
    squares = jnp.sum(factor_prev * factor_prev, axis=1) + jnp.sum(panel_factor * panel_factor, axis=1)
    outgoing = jnp.concatenate([samples, jnp.broadcast_to(squares[None, :], samples.shape)], axis=1)
    incoming = lax.all_to_all(outgoing, ("narrow", "wide"), split_axis=0, concat_axis=0, tiled=True)
    whole = jnp.sum(incoming.reshape(narrow, wide, 2 * row_count), axis=0)
    scaled = whole[:, :row_count] * lax.rsqrt(whole[:, row_count:] + 1e-06)
    uniforms = 0.5 * (1.0 + lax.erf(scaled * HALF_ROOT))
    return (panel_factor, smooth(uniforms.reshape(1, wide * row_count)))


def solution(mesh):
    wide, narrow = mesh.shape["wide"], mesh.shape["narrow"]
    in_specs = (
        P("wide", "narrow"),
        P("wide", "narrow"),
        P("narrow", None),
        P("narrow", None),
        P("narrow", None),
    )
    out_specs = (P("wide", "narrow"), P(("narrow", "wide"), None))

    def body(*blocks):
        return per_device(wide, narrow, *blocks)

    return jax.shard_map(body, mesh=mesh, in_specs=in_specs, out_specs=out_specs, check_vma=False)
```

```python
import math

import jax
import jax.numpy as jnp
from jax import lax
from jax.sharding import PartitionSpec as P

WIN = 5
PRECISE = lax.Precision.HIGH
HALF_ROOT = 1.0 / math.sqrt(2.0)


def contract(left_side, right_side, left_dim, right_dim):
    return lax.dot_general(
        left_side,
        right_side,
        (((left_dim,), (right_dim,)), ((), ())),
        precision=PRECISE,
        preferred_element_type=jnp.float32,
    )


def pack(block, width):
    groups = width // block.shape[1]
    return jnp.concatenate(jnp.split(block, groups, 0), 1)


def unpack(packed, depth):
    return jnp.concatenate(jnp.split(packed, packed.shape[1] // depth, 1), 0)


def broadcast(block, source, wide, narrow, riders):
    place = lax.axis_index("wide")
    on_core = place % 2 == source % 2
    riders, carried = list(riders), []
    packed = pack(block, riders[0][0].shape[1])
    half = packed.shape[0] // 2
    held = jnp.where(place == source, packed, 0.0)
    holders = [source]

    def send(value, to):
        pairs = [(h * narrow + i, (h ^ to) * narrow + i) for h in holders for i in range(narrow)]
        if not riders or value.shape != riders[0][0].shape:
            return lax.ppermute(value, ("wide", "narrow"), pairs)
        rider, more = riders.pop(0)
        carried.append(lax.ppermute(jnp.where(on_core, value, rider), ("wide", "narrow"), pairs + more))
        return carried[-1]

    shift = 1
    while (1 << shift) < wide:
        low, high, both = 1 << shift, 2 << shift, 3 << shift
        top, bottom = packed[:half], packed[half:]
        got = {}
        if high < wide:
            got['TL'] = send(top, low)
            got['TD'] = send(top, both)
            got['TH'] = send(top, high)
            got['BD'] = send(bottom, both)
            got['BL'] = send(bottom, low)
            got['BH'] = send(bottom, high)
            tops, bottoms = [got['TD'], got['TL'], got['TH']], [got['BD'], got['BL'], got['BH']]
        else:
            tops, bottoms = [send(top, low)], [send(bottom, low)]
        held = held + jnp.concatenate([sum(tops), sum(bottoms)])
        holders = [h ^ f for h in holders for f in (0, low, high, both)[: 1 + len(tops)]]
        packed = held
        shift += 2
    return held, carried


def smooth(uniforms):
    half_span = (WIN - 1) // 2
    feature_count = uniforms.shape[1]
    padded = jnp.pad(uniforms, ((0, 0), (half_span, half_span)))
    summed = jnp.zeros_like(uniforms)
    for offset in range(WIN):
        weight_tap = math.comb(WIN - 1, offset) / 2.0 ** (WIN - 1)
        summed = summed + weight_tap * padded[:, offset : offset + feature_count]
    return summed


def per_device(wide, narrow, corr_panel, factor_prev, draws_prev, draws_panel, diag_inverse):
    row_count, depth = factor_prev.shape
    col_share, panel = diag_inverse.shape
    narrow_place = lax.axis_index("narrow")
    source = depth * narrow // row_count
    on_core = lax.axis_index("wide") % 2 == source % 2
    fetchers = [c for c in range(wide) if c % 2 != source % 2]

    def shifted(k):
        return [(c * narrow + i, c * narrow + (i + k) % narrow) for c in fetchers for i in range(narrow)]

    far = list(range(narrow - 1, 0, -1))
    own_pivot, rows = broadcast(
        factor_prev, source, wide, narrow, [(diag_inverse, shifted(k)) for k in far]
    )
    rows = dict(zip(far, lax.optimization_barrier(tuple(rows))))

    draws = lax.optimization_barrier(jnp.concatenate([draws_prev, draws_panel]))
    samples_prev = contract(draws[:depth], factor_prev, 0, 1)

    even = narrow_place % 2 == 0
    own_rows = jnp.concatenate(
        [rows[2], jnp.where(even, rows[1], rows[3]), jnp.where(even, rows[3], rows[1])]
    )
    spare = own_rows.shape[0] - own_pivot.shape[0]
    pieces = jnp.where(on_core, jnp.pad(own_pivot, ((0, spare), (0, 0))), own_rows)
    swapped = lax.ppermute(pieces, "wide", [(i, i ^ 1) for i in range(wide)])
    own_pivot, swapped_pivot = pieces[: own_pivot.shape[0]], swapped[: own_pivot.shape[0]]
    pivot = unpack(jnp.where(on_core, own_pivot, swapped_pivot), depth)

    def part(diag, pivot):
        mixed = contract(diag, pivot, 1, 0)
        own_cols = lax.dynamic_slice_in_dim(diag, narrow_place * col_share, col_share, 1)
        return contract(corr_panel, own_cols, 1, 1) - contract(factor_prev, mixed, 1, 1)

    def turn_part(t, pivot):
        at = slice(t * col_share, (t + 1) * col_share)
        return lax.optimization_barrier((part(jnp.where(on_core, swapped[at], pieces[at]), pivot), pivot))

    end = (narrow_place == 0) | (narrow_place == narrow - 1)
    two_on, pivot = turn_part(0, pivot)
    two_on = lax.ppermute(two_on, "narrow", [(0, 1), (1, 3), (2, 0), (3, 2)])
    across, pivot = turn_part(1, pivot)
    beside, pivot = turn_part(2, pivot)
    across, beside = lax.optimization_barrier((across, beside))
    outer = lax.ppermute(across, "narrow", [(0, 3), (3, 0)])
    beside = lax.ppermute(beside, "narrow", [(0, 1), (1, 0), (2, 3), (3, 2)])
    inner = across + two_on
    inner, two_on, pivot = lax.optimization_barrier((inner, two_on, pivot))
    inner = lax.ppermute(inner, "narrow", [(1, 2), (2, 1)])
    parts = part(diag_inverse, pivot) + jnp.where(end, two_on, 0.0) + beside + outer
    panel_factor = lax.optimization_barrier(parts) + inner

    samples = samples_prev + contract(draws[depth:], panel_factor, 0, 1)
    squares = jnp.sum(factor_prev * factor_prev, axis=1) + jnp.sum(panel_factor * panel_factor, axis=1)
    outgoing = jnp.concatenate([samples, jnp.broadcast_to(squares[None, :], samples.shape)], axis=1)
    incoming = lax.all_to_all(outgoing, ("narrow", "wide"), split_axis=0, concat_axis=0, tiled=True)
    whole = jnp.sum(incoming.reshape(narrow, wide, 2 * row_count), axis=0)
    scaled = whole[:, :row_count] * lax.rsqrt(whole[:, row_count:] + 1e-06)
    uniforms = 0.5 * (1.0 + lax.erf(scaled * HALF_ROOT))
    return (panel_factor, smooth(uniforms.reshape(1, wide * row_count)))


def solution(mesh):
    wide, narrow = mesh.shape["wide"], mesh.shape["narrow"]
    in_specs = (
        P("wide", "narrow"),
        P("wide", "narrow"),
        P("narrow", None),
        P("narrow", None),
        P("narrow", None),
    )
    out_specs = (P("wide", "narrow"), P(("narrow", "wide"), None))

    def body(*blocks):
        return per_device(wide, narrow, *blocks)

    return jax.shard_map(body, mesh=mesh, in_specs=in_specs, out_specs=out_specs, check_vma=False)
```

```python
import math

import jax
import jax.numpy as jnp
from jax import lax
from jax.sharding import PartitionSpec as P

WIN = 5
PRECISE = lax.Precision.HIGH
HALF_ROOT = 1.0 / math.sqrt(2.0)


def contract(left_side, right_side, left_dim, right_dim):
    return lax.dot_general(
        left_side,
        right_side,
        (((left_dim,), (right_dim,)), ((), ())),
        precision=PRECISE,
        preferred_element_type=jnp.float32,
    )


def pack(block, width):
    groups = width // block.shape[1]
    return jnp.concatenate(jnp.split(block, groups, 0), 1)


def unpack(packed, depth):
    return jnp.concatenate(jnp.split(packed, packed.shape[1] // depth, 1), 0)


def broadcast(block, source, wide, narrow, riders):
    place = lax.axis_index("wide")
    on_core = place % 2 == source % 2
    riders, carried = list(riders), []
    packed = pack(block, riders[0][0].shape[1])
    half = packed.shape[0] // 2
    held = jnp.where(place == source, packed, 0.0)
    holders = [source]

    def send(value, to):
        pairs = [(h * narrow + i, (h ^ to) * narrow + i) for h in holders for i in range(narrow)]
        if not riders or value.shape != riders[0][0].shape:
            return lax.ppermute(value, ("wide", "narrow"), pairs)
        rider, more = riders.pop(0)
        carried.append(lax.ppermute(jnp.where(on_core, value, rider), ("wide", "narrow"), pairs + more))
        return carried[-1]

    shift = 1
    while (1 << shift) < wide:
        low, high, both = 1 << shift, 2 << shift, 3 << shift
        top, bottom = packed[:half], packed[half:]
        got = {}
        if high < wide:
            got['TL'] = send(top, low)
            got['TD'] = send(top, both)
            got['TH'] = send(top, high)
            got['BD'] = send(bottom, both)
            got['BL'] = send(bottom, low)
            got['BH'] = send(bottom, high)
            tops, bottoms = [got['TD'], got['TL'], got['TH']], [got['BD'], got['BL'], got['BH']]
        else:
            tops, bottoms = [send(top, low)], [send(bottom, low)]
        held = held + jnp.concatenate([sum(tops), sum(bottoms)])
        holders = [h ^ f for h in holders for f in (0, low, high, both)[: 1 + len(tops)]]
        packed = held
        shift += 2
    return held, carried


def smooth(uniforms):
    half_span = (WIN - 1) // 2
    feature_count = uniforms.shape[1]
    padded = jnp.pad(uniforms, ((0, 0), (half_span, half_span)))
    summed = jnp.zeros_like(uniforms)
    for offset in range(WIN):
        weight_tap = math.comb(WIN - 1, offset) / 2.0 ** (WIN - 1)
        summed = summed + weight_tap * padded[:, offset : offset + feature_count]
    return summed


def per_device(wide, narrow, corr_panel, factor_prev, draws_prev, draws_panel, diag_inverse):
    row_count, depth = factor_prev.shape
    col_share, panel = diag_inverse.shape
    narrow_place = lax.axis_index("narrow")
    source = depth * narrow // row_count
    on_core = lax.axis_index("wide") % 2 == source % 2
    fetchers = [c for c in range(wide) if c % 2 != source % 2]

    def shifted(k):
        return [(c * narrow + i, c * narrow + (i + k) % narrow) for c in fetchers for i in range(narrow)]

    far = list(range(narrow - 1, 0, -1))
    own_pivot, rows = broadcast(
        factor_prev, source, wide, narrow, [(diag_inverse, shifted(k)) for k in far]
    )
    rows = dict(zip(far, lax.optimization_barrier(tuple(rows))))

    draws = lax.optimization_barrier(jnp.concatenate([draws_prev, draws_panel]))
    samples_prev = contract(draws[:depth], factor_prev, 0, 1)

    even = narrow_place % 2 == 0
    own_rows = jnp.concatenate(
        [rows[2], jnp.where(even, rows[1], rows[3]), jnp.where(even, rows[3], rows[1])]
    )
    spare = own_rows.shape[0] - own_pivot.shape[0]
    pieces = jnp.where(on_core, jnp.pad(own_pivot, ((0, spare), (0, 0))), own_rows)
    swapped = lax.ppermute(pieces, "wide", [(i, i ^ 1) for i in range(wide)])
    own_pivot, swapped_pivot = pieces[: own_pivot.shape[0]], swapped[: own_pivot.shape[0]]
    pivot = unpack(jnp.where(on_core, own_pivot, swapped_pivot), depth)

    def part(diag, pivot):
        mixed = contract(diag, pivot, 1, 0)
        own_cols = lax.dynamic_slice_in_dim(diag, narrow_place * col_share, col_share, 1)
        return contract(corr_panel, own_cols, 1, 1) - contract(factor_prev, mixed, 1, 1)

    def turn_part(t, pivot):
        at = slice(t * col_share, (t + 1) * col_share)
        return lax.optimization_barrier((part(jnp.where(on_core, swapped[at], pieces[at]), pivot), pivot))

    end = (narrow_place == 0) | (narrow_place == narrow - 1)
    two_on, pivot = turn_part(0, pivot)
    two_on = lax.ppermute(two_on, "narrow", [(0, 1), (1, 3), (2, 0), (3, 2)])
    beside, pivot = turn_part(2, pivot)
    across, pivot = turn_part(1, pivot)
    across, beside = lax.optimization_barrier((across, beside))
    outer = lax.ppermute(across, "narrow", [(0, 3), (3, 0)])
    beside = lax.ppermute(beside, "narrow", [(0, 1), (1, 0), (2, 3), (3, 2)])
    inner = across + two_on
    inner, two_on, pivot = lax.optimization_barrier((inner, two_on, pivot))
    inner = lax.ppermute(inner, "narrow", [(1, 2), (2, 1)])
    parts = part(diag_inverse, pivot) + jnp.where(end, two_on, 0.0) + beside + outer
    panel_factor = lax.optimization_barrier(parts) + inner

    samples = samples_prev + contract(draws[depth:], panel_factor, 0, 1)
    squares = jnp.sum(factor_prev * factor_prev, axis=1) + jnp.sum(panel_factor * panel_factor, axis=1)
    count, lanes = samples.shape[0], 128
    groups = row_count // lanes
    outgoing = jnp.concatenate(
        [
            samples.reshape(count, groups, lanes),
            jnp.broadcast_to(squares.reshape(1, groups, lanes), (count, groups, lanes)),
        ],
        axis=1,
    )
    incoming = lax.all_to_all(outgoing, ("narrow", "wide"), split_axis=0, concat_axis=0, tiled=True)
    whole = jnp.sum(incoming.reshape(narrow, wide, 2 * groups, lanes), axis=0)
    scaled = whole[:, :groups] * lax.rsqrt(whole[:, groups:] + 1e-06)
    uniforms = 0.5 * (1.0 + lax.erf(scaled * HALF_ROOT))
    return (panel_factor, smooth(uniforms.reshape(1, wide * row_count)))


def solution(mesh):
    wide, narrow = mesh.shape["wide"], mesh.shape["narrow"]
    in_specs = (
        P("wide", "narrow"),
        P("wide", "narrow"),
        P("narrow", None),
        P("narrow", None),
        P("narrow", None),
    )
    out_specs = (P("wide", "narrow"), P(("narrow", "wide"), None))

    def body(*blocks):
        return per_device(wide, narrow, *blocks)

    return jax.shard_map(body, mesh=mesh, in_specs=in_specs, out_specs=out_specs, check_vma=False)
```

```python
import math

import jax
import jax.numpy as jnp
from jax import lax
from jax.sharding import PartitionSpec as P

WIN = 5
PRECISE = lax.Precision.HIGH
HALF_ROOT = 1.0 / math.sqrt(2.0)


def contract(left_side, right_side, left_dim, right_dim):
    return lax.dot_general(
        left_side,
        right_side,
        (((left_dim,), (right_dim,)), ((), ())),
        precision=PRECISE,
        preferred_element_type=jnp.float32,
    )


def pack(block, width):
    groups = width // block.shape[1]
    return jnp.concatenate(jnp.split(block, groups, 0), 1)


def unpack(packed, depth):
    return jnp.concatenate(jnp.split(packed, packed.shape[1] // depth, 1), 0)


def broadcast(block, source, wide, narrow, riders):
    place = lax.axis_index("wide")
    on_core = place % 2 == source % 2
    riders, carried = list(riders), []
    packed = pack(block, riders[0][0].shape[1])
    half = packed.shape[0] // 2
    held = jnp.where(place == source, packed, 0.0)
    holders = [source]

    def send(value, to, fro=0):
        pairs = [((h ^ fro) * narrow + i, (h ^ to) * narrow + i) for h in holders for i in range(narrow)]
        if not riders:
            return lax.ppermute(value, ("wide", "narrow"), pairs)
        rider, more = riders.pop(0)
        carried.append(lax.ppermute(jnp.where(on_core, value, rider), ("wide", "narrow"), pairs + more))
        return carried[-1]

    shift = 1
    while (1 << shift) < wide:
        low, high, both = 1 << shift, 2 << shift, 3 << shift
        top, bottom = packed[:half], packed[half:]
        low_top = send(top, low)
        if high < wide:
            high_bottom = send(bottom, high)
            high_top = send(top, high)
            both_bottom = send(bottom, both)
        low_bottom = send(bottom, low)
        tops, bottoms = low_top, low_bottom
        if high < wide:
            both_top = send(low_top, both, low)
            tops, bottoms = both_top + low_top + high_top, both_bottom + low_bottom + high_bottom
        held = held + jnp.concatenate([tops, bottoms])
        holders = [h ^ f for h in holders for f in ((0, low, high, both) if high < wide else (0, low))]
        packed = held
        shift += 2
    return held, carried


def smooth(uniforms):
    half_span = (WIN - 1) // 2
    feature_count = uniforms.shape[1]
    padded = jnp.pad(uniforms, ((0, 0), (half_span, half_span)))
    summed = jnp.zeros_like(uniforms)
    for offset in range(WIN):
        weight_tap = math.comb(WIN - 1, offset) / 2.0 ** (WIN - 1)
        summed = summed + weight_tap * padded[:, offset : offset + feature_count]
    return summed


def per_device(wide, narrow, corr_panel, factor_prev, draws_prev, draws_panel, diag_inverse):
    row_count, depth = factor_prev.shape
    col_share, panel = diag_inverse.shape
    narrow_place = lax.axis_index("narrow")
    source = depth * narrow // row_count
    on_core = lax.axis_index("wide") % 2 == source % 2
    fetchers = [c for c in range(wide) if c % 2 != source % 2]

    def shifted(k):
        return [(c * narrow + i, c * narrow + (i ^ k)) for c in fetchers for i in range(narrow)]

    far = [2, 1, 3]
    own_pivot, rows = broadcast(
        factor_prev, source, wide, narrow, [(diag_inverse, shifted(k)) for k in far]
    )
    rows = dict(zip(far, lax.optimization_barrier(tuple(rows))))

    draws = lax.optimization_barrier(jnp.concatenate([draws_prev, draws_panel]))
    samples_prev = contract(draws[:depth], factor_prev, 0, 1)

    own_rows = jnp.concatenate([rows[2], rows[3], rows[1]])
    spare = own_rows.shape[0] - own_pivot.shape[0]
    pieces = jnp.where(on_core, jnp.pad(own_pivot, ((0, spare), (0, 0))), own_rows)
    swapped = lax.ppermute(pieces, "wide", [(i, i ^ 1) for i in range(wide)])
    own_pivot, swapped_pivot = pieces[: own_pivot.shape[0]], swapped[: own_pivot.shape[0]]
    pivot = unpack(jnp.where(on_core, own_pivot, swapped_pivot), depth)

    def part(diag, pivot):
        mixed = contract(diag, pivot, 1, 0)
        own_cols = lax.dynamic_slice_in_dim(diag, narrow_place * col_share, col_share, 1)
        return contract(corr_panel, own_cols, 1, 1) - contract(factor_prev, mixed, 1, 1)

    def turn_part(t, pivot):
        at = slice(t * col_share, (t + 1) * col_share)
        return lax.optimization_barrier((part(jnp.where(on_core, swapped[at], pieces[at]), pivot), pivot))

    end = (narrow_place == 0) | (narrow_place == narrow - 1)
    two_on, pivot = turn_part(0, pivot)
    two_on = lax.ppermute(two_on, "narrow", [(0, 1), (1, 3), (2, 0), (3, 2)])
    beside, pivot = turn_part(2, pivot)
    across, pivot = turn_part(1, pivot)
    across, beside = lax.optimization_barrier((across, beside))
    outer = lax.ppermute(across, "narrow", [(0, 3), (3, 0)])
    beside = lax.ppermute(beside, "narrow", [(0, 1), (1, 0), (2, 3), (3, 2)])
    inner = across + two_on
    inner, two_on, pivot = lax.optimization_barrier((inner, two_on, pivot))
    inner = lax.ppermute(inner, "narrow", [(1, 2), (2, 1)])
    parts = part(diag_inverse, pivot) + jnp.where(end, two_on, 0.0) + beside + outer
    panel_factor = lax.optimization_barrier(parts) + inner

    samples = samples_prev + contract(draws[depth:], panel_factor, 0, 1)
    squares = jnp.sum(factor_prev * factor_prev, axis=1) + jnp.sum(panel_factor * panel_factor, axis=1)
    count, lanes = samples.shape[0], 128
    groups = row_count // lanes
    outgoing = jnp.concatenate(
        [
            samples.reshape(count, groups, lanes),
            jnp.broadcast_to(squares.reshape(1, groups, lanes), (count, groups, lanes)),
        ],
        axis=1,
    )
    incoming = lax.all_to_all(outgoing, ("narrow", "wide"), split_axis=0, concat_axis=0, tiled=True)
    whole = jnp.sum(incoming.reshape(narrow, wide, 2 * groups, lanes), axis=0)
    scaled = whole[:, :groups] * lax.rsqrt(whole[:, groups:] + 1e-06)
    uniforms = 0.5 * (1.0 + lax.erf(scaled * HALF_ROOT))
    return (panel_factor, smooth(uniforms.reshape(1, wide * row_count)))


def solution(mesh):
    wide, narrow = mesh.shape["wide"], mesh.shape["narrow"]
    in_specs = (
        P("wide", "narrow"),
        P("wide", "narrow"),
        P("narrow", None),
        P("narrow", None),
        P("narrow", None),
    )
    out_specs = (P("wide", "narrow"), P(("narrow", "wide"), None))

    def body(*blocks):
        return per_device(wide, narrow, *blocks)

    return jax.shard_map(body, mesh=mesh, in_specs=in_specs, out_specs=out_specs, check_vma=False)
```

```python
import math

import jax
import jax.numpy as jnp
from jax import lax
from jax.sharding import PartitionSpec as P

WIN = 5
PRECISE = lax.Precision.HIGH
HALF_ROOT = 1.0 / math.sqrt(2.0)


def contract(left_side, right_side, left_dim, right_dim):
    return lax.dot_general(
        left_side,
        right_side,
        (((left_dim,), (right_dim,)), ((), ())),
        precision=PRECISE,
        preferred_element_type=jnp.float32,
    )


def pack(block, width):
    groups = width // block.shape[1]
    return jnp.concatenate(jnp.split(block, groups, 0), 1)


def unpack(packed, depth):
    return jnp.concatenate(jnp.split(packed, packed.shape[1] // depth, 1), 0)


def broadcast(block, source, wide, narrow, riders):
    place = lax.axis_index("wide")
    on_core = place % 2 == source % 2
    riders, carried = list(riders), []
    packed = pack(block, riders[0][0].shape[1])
    half = packed.shape[0] // 2
    held = jnp.where(place == source, packed, 0.0)
    holders = [source]

    def send(value, to, fro=0):
        pairs = [((h ^ fro) * narrow + i, (h ^ to) * narrow + i) for h in holders for i in range(narrow)]
        if not riders:
            return lax.ppermute(value, ("wide", "narrow"), pairs)
        rider, more = riders.pop(0)
        carried.append(lax.ppermute(jnp.where(on_core, value, rider), ("wide", "narrow"), pairs + more))
        return carried[-1]

    shift = 1
    while (1 << shift) < wide:
        low, high, both = 1 << shift, 2 << shift, 3 << shift
        top, bottom = packed[:half], packed[half:]
        low_top = send(top, low)
        if high < wide:
            high_bottom = send(bottom, high)
            both_bottom = send(bottom, both)
            high_top = send(top, high)
        low_bottom = send(bottom, low)
        tops, bottoms = low_top, low_bottom
        if high < wide:
            both_top = send(low_top, both, low)
            tops, bottoms = both_top + low_top + high_top, both_bottom + low_bottom + high_bottom
        held = held + jnp.concatenate([tops, bottoms])
        holders = [h ^ f for h in holders for f in ((0, low, high, both) if high < wide else (0, low))]
        packed = held
        shift += 2
    return held, carried


def smooth(uniforms):
    half_span = (WIN - 1) // 2
    feature_count = uniforms.shape[1]
    padded = jnp.pad(uniforms, ((0, 0), (half_span, half_span)))
    summed = jnp.zeros_like(uniforms)
    for offset in range(WIN):
        weight_tap = math.comb(WIN - 1, offset) / 2.0 ** (WIN - 1)
        summed = summed + weight_tap * padded[:, offset : offset + feature_count]
    return summed


def per_device(wide, narrow, corr_panel, factor_prev, draws_prev, draws_panel, diag_inverse):
    row_count, depth = factor_prev.shape
    col_share, panel = diag_inverse.shape
    narrow_place = lax.axis_index("narrow")
    source = depth * narrow // row_count
    on_core = lax.axis_index("wide") % 2 == source % 2
    fetchers = [c for c in range(wide) if c % 2 != source % 2]

    def shifted(k):
        return [(c * narrow + i, c * narrow + (i ^ k)) for c in fetchers for i in range(narrow)]

    far = [2, 1, 3]
    own_pivot, rows = broadcast(
        factor_prev, source, wide, narrow, [(diag_inverse, shifted(k)) for k in far]
    )
    rows = dict(zip(far, lax.optimization_barrier(tuple(rows))))

    draws = lax.optimization_barrier(jnp.concatenate([draws_prev, draws_panel]))
    samples_prev = contract(draws[:depth], factor_prev, 0, 1)

    own_rows = jnp.concatenate([rows[2], rows[3], rows[1]])
    spare = own_rows.shape[0] - own_pivot.shape[0]
    pieces = jnp.where(on_core, jnp.pad(own_pivot, ((0, spare), (0, 0))), own_rows)
    swapped = lax.ppermute(pieces, "wide", [(i, i ^ 1) for i in range(wide)])
    own_pivot, swapped_pivot = pieces[: own_pivot.shape[0]], swapped[: own_pivot.shape[0]]
    pivot = unpack(jnp.where(on_core, own_pivot, swapped_pivot), depth)

    def part(diag, pivot):
        mixed = contract(diag, pivot, 1, 0)
        own_cols = lax.dynamic_slice_in_dim(diag, narrow_place * col_share, col_share, 1)
        return contract(corr_panel, own_cols, 1, 1) - contract(factor_prev, mixed, 1, 1)

    def turn_part(t, pivot):
        at = slice(t * col_share, (t + 1) * col_share)
        return lax.optimization_barrier((part(jnp.where(on_core, swapped[at], pieces[at]), pivot), pivot))

    end = (narrow_place == 0) | (narrow_place == narrow - 1)
    two_on, pivot = turn_part(0, pivot)
    two_on = lax.ppermute(two_on, "narrow", [(0, 1), (1, 3), (2, 0), (3, 2)])
    across, pivot = turn_part(1, pivot)
    beside, pivot = turn_part(2, pivot)
    across, beside = lax.optimization_barrier((across, beside))
    outer = lax.ppermute(across, "narrow", [(0, 3), (3, 0)])
    beside = lax.ppermute(beside, "narrow", [(0, 1), (1, 0), (2, 3), (3, 2)])
    inner = across + two_on
    inner, two_on, pivot = lax.optimization_barrier((inner, two_on, pivot))
    inner = lax.ppermute(inner, "narrow", [(1, 2), (2, 1)])
    parts = part(diag_inverse, pivot) + jnp.where(end, two_on, 0.0) + beside + outer
    panel_factor = lax.optimization_barrier(parts) + inner

    samples = samples_prev + contract(draws[depth:], panel_factor, 0, 1)
    squares = jnp.sum(factor_prev * factor_prev, axis=1) + jnp.sum(panel_factor * panel_factor, axis=1)
    count, lanes = samples.shape[0], 128
    groups = row_count // lanes
    outgoing = jnp.concatenate(
        [
            samples.reshape(count, groups, lanes),
            jnp.broadcast_to(squares.reshape(1, groups, lanes), (count, groups, lanes)),
        ],
        axis=1,
    )
    incoming = lax.all_to_all(outgoing, ("narrow", "wide"), split_axis=0, concat_axis=0, tiled=True)
    whole = jnp.sum(incoming.reshape(narrow, wide, 2 * groups, lanes), axis=0)
    scaled = whole[:, :groups] * lax.rsqrt(whole[:, groups:] + 1e-06)
    uniforms = 0.5 * (1.0 + lax.erf(scaled * HALF_ROOT))
    return (panel_factor, smooth(uniforms.reshape(1, wide * row_count)))


def solution(mesh):
    wide, narrow = mesh.shape["wide"], mesh.shape["narrow"]
    in_specs = (
        P("wide", "narrow"),
        P("wide", "narrow"),
        P("narrow", None),
        P("narrow", None),
        P("narrow", None),
    )
    out_specs = (P("wide", "narrow"), P(("narrow", "wide"), None))

    def body(*blocks):
        return per_device(wide, narrow, *blocks)

    return jax.shard_map(body, mesh=mesh, in_specs=in_specs, out_specs=out_specs, check_vma=False)
```

```python
import math

import jax
import jax.numpy as jnp
from jax import lax
from jax.sharding import PartitionSpec as P

WIN = 5
PRECISE = lax.Precision.HIGH
HALF_ROOT = 1.0 / math.sqrt(2.0)


def contract(left_side, right_side, left_dim, right_dim):
    return lax.dot_general(
        left_side,
        right_side,
        (((left_dim,), (right_dim,)), ((), ())),
        precision=PRECISE,
        preferred_element_type=jnp.float32,
    )


def pack(block, width):
    groups = width // block.shape[1]
    return jnp.concatenate(jnp.split(block, groups, 0), 1)


def unpack(packed, depth):
    return jnp.concatenate(jnp.split(packed, packed.shape[1] // depth, 1), 0)


def broadcast(block, source, wide, narrow, riders):
    place = lax.axis_index("wide")
    on_core = place % 2 == source % 2
    riders, carried = list(riders), []
    packed = pack(block, riders[0][0].shape[1])
    half = packed.shape[0] // 2
    held = jnp.where(place == source, packed, 0.0)
    holders = [source]

    def send(value, to, fro=0):
        pairs = [((h ^ fro) * narrow + i, (h ^ to) * narrow + i) for h in holders for i in range(narrow)]
        if not riders:
            return lax.ppermute(value, ("wide", "narrow"), pairs)
        rider, more = riders.pop(0)
        carried.append(lax.ppermute(jnp.where(on_core, value, rider), ("wide", "narrow"), pairs + more))
        return carried[-1]

    shift = 1
    while (1 << shift) < wide:
        low, high, both = 1 << shift, 2 << shift, 3 << shift
        top, bottom = packed[:half], packed[half:]
        low_top = send(top, low)
        if high < wide:
            high_bottom = send(bottom, high)
            both_bottom = send(bottom, both)
            high_top = send(top, high)
        low_bottom = send(bottom, low)
        tops, bottoms = low_top, low_bottom
        if high < wide:
            both_top = send(low_top, both, low)
            tops, bottoms = both_top + low_top + high_top, both_bottom + low_bottom + high_bottom
        held = held + jnp.concatenate([tops, bottoms])
        holders = [h ^ f for h in holders for f in ((0, low, high, both) if high < wide else (0, low))]
        packed = held
        shift += 2
    return held, carried


def smooth(uniforms):
    half_span = (WIN - 1) // 2
    feature_count = uniforms.shape[1]
    padded = jnp.pad(uniforms, ((0, 0), (half_span, half_span)))
    summed = jnp.zeros_like(uniforms)
    for offset in range(WIN):
        weight_tap = math.comb(WIN - 1, offset) / 2.0 ** (WIN - 1)
        summed = summed + weight_tap * padded[:, offset : offset + feature_count]
    return summed


def per_device(wide, narrow, corr_panel, factor_prev, draws_prev, draws_panel, diag_inverse):
    row_count, depth = factor_prev.shape
    col_share, panel = diag_inverse.shape
    narrow_place = lax.axis_index("narrow")
    source = depth * narrow // row_count
    on_core = lax.axis_index("wide") % 2 == source % 2
    fetchers = [c for c in range(wide) if c % 2 != source % 2]

    def shifted(k):
        return [(c * narrow + i, c * narrow + (i ^ k)) for c in fetchers for i in range(narrow)]

    far = [2, 1, 3]
    own_pivot, rows = broadcast(
        factor_prev, source, wide, narrow, [(diag_inverse, shifted(k)) for k in far]
    )
    rows = dict(zip(far, rows))

    draws = lax.optimization_barrier(jnp.concatenate([draws_prev, draws_panel]))
    samples_prev = contract(draws[:depth], factor_prev, 0, 1)

    own_rows = jnp.concatenate([rows[2], rows[3], rows[1]])
    spare = own_rows.shape[0] - own_pivot.shape[0]
    pieces = jnp.where(on_core, jnp.pad(own_pivot, ((0, spare), (0, 0))), own_rows)
    swapped = lax.ppermute(pieces, "wide", [(i, i ^ 1) for i in range(wide)])
    own_pivot, swapped_pivot = pieces[: own_pivot.shape[0]], swapped[: own_pivot.shape[0]]
    pivot = unpack(jnp.where(on_core, own_pivot, swapped_pivot), depth)

    def part(diag, pivot):
        mixed = contract(diag, pivot, 1, 0)
        own_cols = lax.dynamic_slice_in_dim(diag, narrow_place * col_share, col_share, 1)
        return contract(corr_panel, own_cols, 1, 1) - contract(factor_prev, mixed, 1, 1)

    def turn_part(t, pivot):
        at = slice(t * col_share, (t + 1) * col_share)
        return lax.optimization_barrier((part(jnp.where(on_core, swapped[at], pieces[at]), pivot), pivot))

    end = (narrow_place == 0) | (narrow_place == narrow - 1)
    two_on, pivot = turn_part(0, pivot)
    two_on = lax.ppermute(two_on, "narrow", [(0, 1), (1, 3), (2, 0), (3, 2)])
    across, pivot = turn_part(1, pivot)
    beside, pivot = turn_part(2, pivot)
    across, beside = lax.optimization_barrier((across, beside))
    outer = lax.ppermute(across, "narrow", [(0, 3), (3, 0)])
    beside = lax.ppermute(beside, "narrow", [(0, 1), (1, 0), (2, 3), (3, 2)])
    inner = across + two_on
    inner, two_on, pivot = lax.optimization_barrier((inner, two_on, pivot))
    inner = lax.ppermute(inner, "narrow", [(1, 2), (2, 1)])
    parts = part(diag_inverse, pivot) + jnp.where(end, two_on, 0.0) + beside + outer
    panel_factor = lax.optimization_barrier(parts) + inner

    samples = samples_prev + contract(draws[depth:], panel_factor, 0, 1)
    squares = jnp.sum(factor_prev * factor_prev, axis=1) + jnp.sum(panel_factor * panel_factor, axis=1)
    count, lanes = samples.shape[0], 128
    groups = row_count // lanes
    outgoing = jnp.concatenate(
        [
            samples.reshape(count, groups, lanes),
            jnp.broadcast_to(squares.reshape(1, groups, lanes), (count, groups, lanes)),
        ],
        axis=1,
    )
    incoming = lax.all_to_all(outgoing, ("narrow", "wide"), split_axis=0, concat_axis=0, tiled=True)
    whole = jnp.sum(incoming.reshape(narrow, wide, 2 * groups, lanes), axis=0)
    scaled = whole[:, :groups] * lax.rsqrt(whole[:, groups:] + 1e-06)
    uniforms = 0.5 * (1.0 + lax.erf(scaled * HALF_ROOT))
    return (panel_factor, smooth(uniforms.reshape(1, wide * row_count)))


def solution(mesh):
    wide, narrow = mesh.shape["wide"], mesh.shape["narrow"]
    in_specs = (
        P("wide", "narrow"),
        P("wide", "narrow"),
        P("narrow", None),
        P("narrow", None),
        P("narrow", None),
    )
    out_specs = (P("wide", "narrow"), P(("narrow", "wide"), None))

    def body(*blocks):
        return per_device(wide, narrow, *blocks)

    return jax.shard_map(body, mesh=mesh, in_specs=in_specs, out_specs=out_specs, check_vma=False)
```
